128 devices in a mesh: gx: 8 (over x_lo, y), gy: 4 (over z), gz: 4 (over x_hi, core).
Axes of the slice: x: 4 (x_hi: 2, x_lo: 2; x = x_hi * 2 + x_lo), y: 4, z: 4, core: 2. Of those that a mesh axis runs over, the one named last changes fastest.
Arguments:
- fields: float32 [5, 64, 512, 512], P(None, 'gz', 'gx', 'gy'), may hold values from -6 to 6
- metrics: float32 [2, 64, 512, 512], P(None, 'gz', 'gx', 'gy'), may hold values from 0.4 to 2.5
- jacobian_x: float32 [5, 5], replicated, may hold values from -2.5 to 2.5
- jacobian_y: float32 [5, 5], replicated, may hold values from -2.5 to 2.5
- pivot_inverse: bfloat16 [5, 5, 64, 512, 512], P(None, None, 'gz', 'gx', 'gy'), may hold values from -0.25 to 1.25, as said below
- lower_blocks: bfloat16 [5, 5, 64, 512, 512], P(None, None, 'gz', 'gx', 'gy'), may hold values from -1.3 to 0.1
- upper_blocks: bfloat16 [5, 5, 64, 512, 512], P(None, None, 'gz', 'gx', 'gy'), may hold values from -1 to 0.1
Outputs:
- new_fields: float32 [5, 64, 512, 512], P(None, 'gz', 'gx', 'gy')
The draws below stay inside these ranges and needn't reach their ends.
Inputs may be any that keep to these rules, and one draw needn't show every extreme that they name: `pivot_inverse`: each 5x5 block is dominated by its diagonal.
All inputs are finite; a program needn't handle non-finite values.
Results may differ from the reference program's by a relative error of at most 0.0003.
Values sent between devices are 32-bit elements; how exact they have to be, the bound alone decides.
A program may use at most 128 MiB of HBM per device.

```python
import math
import jax
import jax.numpy as jnp
from jax import lax

FIELDS = 5
NX = 512
NY = 512
DEPTH_VOLUME_NUM = 64


def common_diagonal(key):
    return jax.random.uniform(jax.random.fold_in(key, 101), (5, DEPTH_VOLUME_NUM, NX, NY), jnp.float32, 0.8, 1.25)


def decay_rates(key, share, slow_low, slow_high):
    keys = jax.random.split(key, 4)
    slow = jax.random.uniform(keys[0], (5, 1, 1, 1)) < share
    ground_tier = jnp.where(slow, jax.random.uniform(keys[1], (5, 1, 1, 1), jnp.float32, slow_low, slow_high), jax.random.uniform(keys[2], (5, 1, 1, 1), jnp.float32, 0.3, 0.6))
    approximate_guess = jax.random.uniform(keys[3], (5, DEPTH_VOLUME_NUM, NX, NY), jnp.float32, 0.95, 1.0)
    packet_batch = jax.random.uniform(jax.random.fold_in(key, 7), (1, DEPTH_VOLUME_NUM, 1, 1)) < 2.5 / DEPTH_VOLUME_NUM
    return ground_tier * approximate_guess * jnp.where(packet_batch, 0.6, 1.0)


def block_matrix(diagonal, key, spread):
    unit_matrix = jnp.eye(5, dtype=jnp.float32)[:, :, None, None, None]
    distribute_entries = jnp.clip(jax.random.normal(key, (5, 5, DEPTH_VOLUME_NUM, NX, NY), jnp.float32) * spread, -3.0 * spread, 3.0 * spread)
    return distribute_entries * (1.0 - unit_matrix) + unit_matrix * diagonal[:, None]


def draw_pivot_inverse(key, part):
    diagonal = common_diagonal(key)
    key = jax.random.fold_in(key, 1)
    return block_matrix(diagonal, key, 0.07).astype(jnp.bfloat16)


def draw_lower_blocks(key, part):
    diagonal = common_diagonal(key)
    key = jax.random.fold_in(key, 2)
    rates = decay_rates(key, 0.6, 0.93, 0.97)
    return block_matrix(-rates / diagonal, jax.random.fold_in(key, 9), 0.03).astype(jnp.bfloat16)


def draw_upper_blocks(key, part):
    key = jax.random.fold_in(key, 3)
    rates = decay_rates(key, 0.6, 0.93, 0.97)
    return block_matrix(-rates, jax.random.fold_in(key, 9), 0.03).astype(jnp.bfloat16)


def shard_levels(own_key, shape, cuts, low, top_value):
    level = 1.0
    for position, blocks in cuts:
        draws = jax.random.uniform(jax.random.fold_in(jax.random.fold_in(own_key, 6), position), (blocks,), jnp.float32, low / len(cuts), top_value / len(cuts))
        level = level * jnp.repeat(jnp.exp(draws), shape[position] // blocks).reshape((-1,) + (1,) * (len(shape) - 1 - position))
    return level


def gaussian(own_key, extent, width, limit, pieces=(), kind=jnp.bfloat16):
    entries = width * jax.random.normal(own_key, extent, jnp.float32)
    if pieces:
        entries = entries * shard_levels(own_key, extent, pieces, -0.22, 0.18)
    return jnp.clip(entries, -limit, limit).astype(kind)


def setup_inputs(seed: int = 0) -> dict:
    seeds = jax.random.split(jax.random.key(seed), 8)
    fields = gaussian(seeds[0], (FIELDS, DEPTH_VOLUME_NUM, NX, NY), 1.0, 6.0, ((1, 4), (2, 8), (3, 4)), jnp.float32)
    metrics = jnp.clip(jnp.exp(math.log(2.5) - 1.8325814 * jax.random.uniform(seeds[1], (2, DEPTH_VOLUME_NUM, NX, NY), jnp.float32) ** shard_levels(seeds[1], (2, DEPTH_VOLUME_NUM, NX, NY), ((1, 4), (2, 8), (3, 4)), -0.2, 0.2)), 0.4, 2.5)
    jacobian_x = gaussian(seeds[2], (FIELDS, FIELDS), FIELDS ** -0.5, 2.5, (), jnp.float32)
    jacobian_y = gaussian(seeds[3], (FIELDS, FIELDS), FIELDS ** -0.5, 2.5, (), jnp.float32)
    pivot_inverse = draw_pivot_inverse(jax.random.fold_in(seeds[7], 71), 0)
    lower_blocks = draw_lower_blocks(jax.random.fold_in(seeds[7], 71), 0)
    upper_blocks = draw_upper_blocks(jax.random.fold_in(seeds[7], 71), 0)
    return {"fields": fields, "metrics": metrics, "jacobian_x": jacobian_x, "jacobian_y": jacobian_y, "pivot_inverse": pivot_inverse, "lower_blocks": lower_blocks, "upper_blocks": upper_blocks}


STEP = 0.25


def apply_block(matrix, vector):
    return jnp.stack([sum(matrix[i][j] * vector[j] for j in range(5)) for i in range(5)])


def fourth_diff(padded, axis):
    number = padded.shape[axis] - 4

    def plane(start):
        return lax.slice_in_dim(padded, start, start + number, axis=axis)

    return (plane(0) - plane(4) + 8.0 * (plane(3) - plane(1))) / 12.0


def reference(fields, metrics, jacobian_x, jacobian_y, pivot_inverse, lower_blocks, upper_blocks):
    flux_x = metrics[0] * apply_block(jacobian_x, fields)
    flux_y = metrics[1] * apply_block(jacobian_y, fields)
    x_padded_field = jnp.pad(flux_x, ((0, 0), (0, 0), (2, 2), (0, 0)))
    padded_y = jnp.pad(flux_y, ((0, 0), (0, 0), (0, 0), (2, 2)))
    forcing = -STEP * (fourth_diff(x_padded_field, 2) + fourth_diff(padded_y, 3))

    def forward(carried, plane):
        source = lax.dynamic_index_in_dim(forcing, plane, 1, keepdims=False)
        pivot = lax.dynamic_index_in_dim(pivot_inverse, plane, 2, keepdims=False).astype(jnp.float32)
        lower = lax.dynamic_index_in_dim(lower_blocks, plane, 2, keepdims=False).astype(jnp.float32)
        result = apply_block(pivot, source - apply_block(lower, carried))
        return result, result

    start = jnp.zeros((5, NX, NY), jnp.float32)
    indices = jnp.arange(DEPTH_VOLUME_NUM, dtype=jnp.int32)
    _, forward_planes = lax.scan(forward, start, indices)

    def reversed_pass(carried, plane):
        source = lax.dynamic_index_in_dim(forward_planes, plane, 0, keepdims=False)
        upper = lax.dynamic_index_in_dim(upper_blocks, plane, 2, keepdims=False).astype(jnp.float32)
        result = source - apply_block(upper, carried)
        return result, result

    _, update_planes = lax.scan(reversed_pass, start, indices, reverse=True)
    return fields + jnp.transpose(update_planes, (1, 0, 2, 3))
```

```python
import jax
import jax.numpy as jnp
from jax import lax
from jax.experimental import pallas as pl
from jax.experimental.pallas import tpu as pltpu
from jax.sharding import PartitionSpec as P

STEP = 0.25
SCALE = -STEP / 12.0
CHUNK = 16
LANES = 128
F32 = jnp.float32
BF16 = jnp.bfloat16


def sum_of(terms):
    total = terms[0]
    for term in terms[1:]:
        total = total + term
    return total


def kernel(
    fields, metrics, jx, jy, pivot, lower, upper, out,
    cells, pv, lo, up, fx, w, result, band,
    xsend, xrecv, ysend, yrecv, corr, up_send, up_recv, down_send, down_recv,
    cell_sem, block_sem, out_sem, halo_ssem, halo_rsem, up_ssem, up_rsem, down_ssem, down_rsem,
):
    depth, rows = fields.shape[1], fields.shape[2]
    chunks = rows // CHUNK
    gx, gy, gz = lax.axis_index("gx"), lax.axis_index("gy"), lax.axis_index("gz")
    nx, ny, nz = lax.axis_size("gx"), lax.axis_size("gy"), lax.axis_size("gz")

    cell_copies = []
    for v in range(7):
        source = fields.at[v] if v < 5 else metrics.at[v - 5]
        cell_copies.append(pltpu.make_async_copy(source, cells.at[v], cell_sem.at[v]))
    for copy in cell_copies:
        copy.start()
    block_copies = {}
    for kind, (source, target) in enumerate(((lower, lo), (pivot, pv), (upper, up))):
        for c in range(chunks):
            part = pl.ds(c * CHUNK, CHUNK)
            block_copies[kind, c] = pltpu.make_async_copy(
                source.at[:, :, :, part, :], target.at[:, :, :, part, :], block_sem.at[kind, c]
            )
    for c in range(chunks):
        block_copies[0, c].start()
        block_copies[1, c].start()
    for c in range(chunks):
        block_copies[2, c].start()

    barrier = pltpu.get_barrier_semaphore()
    number = jnp.int32(0)
    for axis, place, size in (("gx", gx, nx), ("gy", gy, ny), ("gz", gz, nz)):
        @pl.when(place > 0)
        def _():
            pl.semaphore_signal(barrier, inc=1, device_id={axis: place - 1}, device_id_type=pl.DeviceIdType.MESH)

        @pl.when(place < size - 1)
        def _():
            pl.semaphore_signal(barrier, inc=1, device_id={axis: place + 1}, device_id_type=pl.DeviceIdType.MESH)

        number = number + jnp.where(place > 0, 1, 0) + jnp.where(place < size - 1, 1, 0)

    def halo_copy(which, target):
        source, destination = ((xsend, xrecv), (ysend, yrecv))[which // 2]
        axis = ("gx", "gy")[which // 2]
        return pltpu.make_async_remote_copy(
            src_ref=source.at[which % 2], dst_ref=destination.at[which % 2],
            send_sem=halo_ssem.at[which], recv_sem=halo_rsem.at[which],
            device_id={axis: target}, device_id_type=pl.DeviceIdType.MESH,
        )

    halos = []
    for which, (place, size) in enumerate(((gx, nx), (gx, nx), (gy, ny), (gy, ny))):
        upward = which % 2 == 0
        copy = halo_copy(which, place + 1 if upward else place - 1)
        sends = place < size - 1 if upward else place > 0
        receives = place > 0 if upward else place < size - 1
        halos.append((copy, sends, receives))

    def up_copy(c):
        return pltpu.make_async_remote_copy(
            src_ref=up_send.at[c], dst_ref=up_recv.at[c], send_sem=up_ssem.at[c], recv_sem=up_rsem.at[c],
            device_id={"gz": gz + 1}, device_id_type=pl.DeviceIdType.MESH,
        )

    def down_copy(c):
        return pltpu.make_async_remote_copy(
            src_ref=down_send.at[c], dst_ref=down_recv.at[c], send_sem=down_ssem.at[c], recv_sem=down_rsem.at[c],
            device_id={"gz": gz - 1}, device_id_type=pl.DeviceIdType.MESH,
        )

    @pl.when(gx == 0)
    def _():
        xrecv[0] = jnp.zeros(xrecv.shape[1:], F32)

    @pl.when(gx == nx - 1)
    def _():
        xrecv[1] = jnp.zeros(xrecv.shape[1:], F32)

    @pl.when(gy == 0)
    def _():
        yrecv[0] = jnp.zeros(yrecv.shape[1:], F32)

    @pl.when(gy == ny - 1)
    def _():
        yrecv[1] = jnp.zeros(yrecv.shape[1:], F32)

    @pl.when(gz == 0)
    def _():
        up_recv[...] = jnp.zeros(up_recv.shape, F32)

    @pl.when(gz == nz - 1)
    def _():
        down_recv[...] = jnp.zeros(down_recv.shape, F32)

    k = lax.broadcasted_iota(jnp.int32, (2 * LANES, LANES), 0)
    j = lax.broadcasted_iota(jnp.int32, (2 * LANES, LANES), 1)
    d = (j - k) & (LANES - 1)
    weight = jnp.where(d == 2, 1.0, 0.0) - jnp.where(d == LANES - 2, 1.0, 0.0)
    weight = weight + jnp.where(d == LANES - 1, 8.0, 0.0) - jnp.where(d == 1, 8.0, 0.0)
    band[...] = weight.astype(BF16)

    for copy in cell_copies:
        copy.wait()

    def pack_x(v, carry):
        for z in range(depth):
            xsend[0, v, 2 * z : 2 * z + 2, :] = cells[v, z, rows - 2 : rows, :]
            xsend[1, v, 2 * z : 2 * z + 2, :] = cells[v, z, 0:2, :]
        return carry

    lax.fori_loop(0, 6, pack_x, 0)
    pl.semaphore_wait(barrier, number)
    for which in (0, 1):
        copy, sends, _ = halos[which]
        pl.when(sends)(copy.start)

    lane = lax.broadcasted_iota(jnp.int32, (CHUNK, LANES), 1)
    pair = lane >> 1

    def pack_y(v, carry):
        low = jnp.zeros((CHUNK, LANES), F32)
        high = low
        for c in range(chunks):
            for z in range(depth):
                slot = CHUNK * c + z
                rolled = cells[v + v // 5, z, c * CHUNK : (c + 1) * CHUNK, :]
                if slot:
                    rolled = pltpu.roll(rolled, 2 * slot, 1)
                low = jnp.where(pair == slot, rolled, low)
                high = jnp.where(pair == (slot - 1) % (LANES // 2), rolled, high)
        ysend[0, v] = high
        ysend[1, v] = low
        return carry

    lax.fori_loop(0, 6, pack_y, 0)
    for which in (2, 3):
        copy, sends, _ = halos[which]
        pl.when(sends)(copy.start)

    jacobian_x = [[jx[i, j] for j in range(5)] for i in range(5)]
    jacobian_y = [[jy[i, j] for j in range(5)] for i in range(5)]

    def flux(jacobian, values, metric):
        factor = metric * SCALE
        return [factor * sum_of([jacobian[i][j] * values[j] for j in range(5)]) for i in range(5)]

    def x_plane(z, carry):
        for c in range(chunks):
            part = pl.ds(c * CHUNK, CHUNK)
            values = flux(jacobian_x, [cells[j, z, part, :] for j in range(5)], cells[5, z, part, :])
            for i in range(5):
                fx[i, z, 8 + c * CHUNK : 8 + (c + 1) * CHUNK, :] = values[i]
        return carry

    lax.fori_loop(0, depth, x_plane, 0)

    def y_plane(z, carry):
        stacks = []
        for c in range(chunks):
            part = pl.ds(c * CHUNK, CHUNK)
            values = flux(jacobian_y, [cells[j, z, part, :] for j in range(5)], cells[6, z, part, :])
            for value in values:
                first = value.astype(BF16)
                second = (value - first.astype(F32)).astype(BF16)
                stacks.append(jnp.concatenate([first, second], 1))
        product = jnp.dot(jnp.concatenate(stacks, 0), band[...], preferred_element_type=F32)
        for c in range(chunks):
            for i in range(5):
                at = (c * 5 + i) * CHUNK
                w[i, z, c * CHUNK : (c + 1) * CHUNK, :] = product[at : at + CHUNK, :]
        return carry

    lax.fori_loop(0, depth, y_plane, 0)

    for copy, _, receives in halos:
        pl.when(receives)(copy.wait_recv)

    for side in range(2):
        values = flux(jacobian_x, [xrecv[side, j] for j in range(5)], xrecv[side, 5])
        for i in range(5):
            for z in range(depth):
                start = 6 if side == 0 else 8 + rows
                fx[i, z, start : start + 2, :] = values[i][2 * z : 2 * z + 2, :]

    theirs = [flux(jacobian_y, [yrecv[s, j] for j in range(5)], yrecv[s, 5]) for s in range(2)]
    mine = [flux(jacobian_y, [ysend[s, j] for j in range(5)], ysend[s, 5]) for s in range(2)]
    odd = (lane & 1) == 1
    upper_pair = (lane & 2) == 2
    for i in range(5):
        high = theirs[0][i] - mine[0][i]
        low = theirs[1][i] - mine[1][i]
        at_start = high - jnp.where(odd, 0.0, 8.0 * pltpu.roll(high, LANES - 1, 1))
        at_end = jnp.where(odd, 8.0 * pltpu.roll(low, 1, 1), 0.0) - low
        at_end = pltpu.roll(at_end, LANES - 4, 1)
        corr[0, i] = jnp.where(upper_pair, at_start, at_end)
        corr[1, i] = jnp.where(upper_pair, at_end, at_start)

    edge = (lane < 2) | (lane >= LANES - 2)

    def force(c):
        base = 8 + c * CHUNK

        def plane(z, carry):
            shift = (2 + 2 * LANES - 2 * CHUNK * c - 2 * z) & (LANES - 1)
            for i in range(5):
                below2 = fx[i, z, base - 2 : base - 2 + CHUNK, :]
                below1 = fx[i, z, base - 1 : base - 1 + CHUNK, :]
                above1 = fx[i, z, base + 1 : base + 1 + CHUNK, :]
                above2 = fx[i, z, base + 2 : base + 2 + CHUNK, :]
                extra = jnp.where(edge, pltpu.roll(corr[z & 1, i], shift, 1), 0.0)
                at = (i, z, pl.ds(c * CHUNK, CHUNK), slice(None))
                w[at] = w[at] + extra + ((below2 - above2) + 8.0 * (above1 - below1))
            return carry

        lax.fori_loop(0, depth, plane, 0)

    def ahead(c):
        part = pl.ds(c * CHUNK, CHUNK)
        block_copies[0, c].wait()
        block_copies[1, c].wait()

        pl.when(gz > 0)(up_copy(c).wait_recv)

        def plane(z, carried):
            inner = []
            for i in range(5):
                total = w[i, z, part, :]
                for j in range(5):
                    total = total - lo[i, j, z, part, :].astype(F32) * carried[j]
                inner.append(total)
            result_here = []
            for i in range(5):
                total = sum_of([pv[i, j, z, part, :].astype(F32) * inner[j] for j in range(5)])
                w[i, z, part, :] = total
                result_here.append(total)
            return tuple(result_here)

        carried = lax.fori_loop(0, depth, plane, tuple(up_recv[c, i] for i in range(5)))
        for i in range(5):
            up_send[c, i] = carried[i]
        pl.when(gz < nz - 1)(up_copy(c).start)

    def out_copy(c):
        part = pl.ds(c * CHUNK, CHUNK)
        return pltpu.make_async_copy(result.at[:, :, part, :], out.at[:, :, part, :], out_sem.at[c])

    def back(c):
        part = pl.ds(c * CHUNK, CHUNK)
        pl.when(gz < nz - 1)(down_copy(c).wait_recv)

        def plane(step, carried):
            z = depth - 1 - step
            new = []
            for i in range(5):
                total = w[i, z, part, :]
                for j in range(5):
                    total = total - up[i, j, z, part, :].astype(F32) * carried[j]
                result[i, z, part, :] = cells[i, z, part, :] + total
                new.append(total)
            return tuple(new)

        carried = lax.fori_loop(0, depth, plane, tuple(down_recv[c, i] for i in range(5)))
        for i in range(5):
            down_send[c, i] = carried[i]
        pl.when(gz > 0)(down_copy(c).start)
        out_copy(c).start()

    @pl.when(gz > 0)
    def _():
        for c in range(chunks):
            force(c)

    for c in range(chunks):
        @pl.when(gz == 0)
        def _():
            force(c)

        ahead(c)

        @pl.when(gz == nz - 1)
        def _():
            block_copies[2, c].wait()
            back(c)

    @pl.when(gz < nz - 1)
    def _():
        for c in range(chunks):
            block_copies[2, c].wait()
            back(c)

    for c in range(chunks):
        out_copy(c).wait()
        pl.when(gz < nz - 1)(up_copy(c).wait_send)
        pl.when(gz > 0)(down_copy(c).wait_send)
    for copy, sends, _ in halos:
        pl.when(sends)(copy.wait_send)


def local(fields, metrics, jacobian_x, jacobian_y, pivot_inverse, lower_blocks, upper_blocks):
    _, depth, rows, columns = fields.shape
    chunks = rows // CHUNK
    anywhere = pl.BlockSpec(memory_space=pl.ANY)
    scalars = pl.BlockSpec(memory_space=pltpu.SMEM)
    dma = pltpu.SemaphoreType.DMA
    return pl.pallas_call(
        kernel,
        out_shape=jax.ShapeDtypeStruct(fields.shape, F32),
        in_specs=[anywhere, anywhere, scalars, scalars, anywhere, anywhere, anywhere],
        out_specs=anywhere,
        scratch_shapes=[
            pltpu.VMEM((7, depth, rows, columns), F32),
            pltpu.VMEM(pivot_inverse.shape, BF16),
            pltpu.VMEM(pivot_inverse.shape, BF16),
            pltpu.VMEM(pivot_inverse.shape, BF16),
            pltpu.VMEM((5, depth, rows + 16, columns), F32),
            pltpu.VMEM(fields.shape, F32),
            pltpu.VMEM(fields.shape, F32),
            pltpu.VMEM((2 * LANES, LANES), BF16),
            pltpu.VMEM((2, 6, 2 * depth, columns), F32),
            pltpu.VMEM((2, 6, 2 * depth, columns), F32),
            pltpu.VMEM((2, 6, CHUNK, LANES), F32),
            pltpu.VMEM((2, 6, CHUNK, LANES), F32),
            pltpu.VMEM((2, 5, CHUNK, LANES), F32),
            pltpu.VMEM((chunks, 5, CHUNK, LANES), F32),
            pltpu.VMEM((chunks, 5, CHUNK, LANES), F32),
            pltpu.VMEM((chunks, 5, CHUNK, LANES), F32),
            pltpu.VMEM((chunks, 5, CHUNK, LANES), F32),
            dma((7,)),
            dma((3, chunks)),
            dma((chunks,)),
            dma((4,)),
            dma((4,)),
            dma((chunks,)),
            dma((chunks,)),
            dma((chunks,)),
            dma((chunks,)),
        ],
        compiler_params=pltpu.CompilerParams(
            collective_id=0, has_side_effects=True, vmem_limit_bytes=48 * 1024 * 1024
        ),
    )(fields, metrics, jacobian_x, jacobian_y, pivot_inverse, lower_blocks, upper_blocks)


def solution(mesh):
    cells = P(None, "gz", "gx", "gy")
    blocks = P(None, None, "gz", "gx", "gy")
    return jax.shard_map(
        local, mesh=mesh, in_specs=(cells, cells, P(), P(), blocks, blocks, blocks),
        out_specs=cells, check_vma=False,
    )
```

```python
import jax
import jax.numpy as jnp
from jax import lax
from jax.experimental import pallas as pl
from jax.experimental.pallas import tpu as pltpu
from jax.sharding import PartitionSpec as P

STEP = 0.25
SCALE = -STEP / 12.0
CHUNK = 16
LANES = 128
F32 = jnp.float32
BF16 = jnp.bfloat16
VMEM_LIMIT = 48 * 1024 * 1024


def sum_of(terms):
    total = terms[0]
    for term in terms[1:]:
        total = total + term
    return total


def kernel(
    fields, metrics, jacobian_x, jacobian_y, pivot, lower, upper, out,
    jx, jy, cells, pv, lo, up, fx, w, result, band,
    xsend, xrecv, ysend, yrecv, corr, up_send, up_recv, down_send, down_recv,
    jacobian_sem, cell_sem, block_sem, out_sem, halo_ssem, halo_rsem, up_ssem, up_rsem, down_ssem, down_rsem,
):
    depth, rows = fields.shape[1], fields.shape[2]
    chunks = rows // CHUNK
    gx, gy, gz = lax.axis_index("gx"), lax.axis_index("gy"), lax.axis_index("gz")
    nx, ny, nz = lax.axis_size("gx"), lax.axis_size("gy"), lax.axis_size("gz")

    cell_copies = [
        pltpu.make_async_copy(jacobian_x, jx, jacobian_sem.at[0]),
        pltpu.make_async_copy(jacobian_y, jy, jacobian_sem.at[1]),
    ]
    for v in range(7):
        source = fields.at[v] if v < 5 else metrics.at[v - 5]
        cell_copies.append(pltpu.make_async_copy(source, cells.at[v], cell_sem.at[v]))
    for copy in cell_copies:
        copy.start()
    block_copies = {}
    for kind, (source, target) in enumerate(((lower, lo), (pivot, pv), (upper, up))):
        for c in range(chunks):
            part = pl.ds(c * CHUNK, CHUNK)
            block_copies[kind, c] = pltpu.make_async_copy(
                source.at[:, :, :, part, :], target.at[:, :, :, part, :], block_sem.at[kind, c]
            )
    for c in range(chunks):
        block_copies[0, c].start()
        block_copies[1, c].start()
    for c in range(chunks):
        block_copies[2, c].start()

    barrier = pltpu.get_barrier_semaphore()
    number = jnp.int32(0)
    for axis, place, size in (("gx", gx, nx), ("gy", gy, ny), ("gz", gz, nz)):
        @pl.when(place > 0)
        def _():
            pl.semaphore_signal(barrier, inc=1, device_id={axis: place - 1}, device_id_type=pl.DeviceIdType.MESH)

        @pl.when(place < size - 1)
        def _():
            pl.semaphore_signal(barrier, inc=1, device_id={axis: place + 1}, device_id_type=pl.DeviceIdType.MESH)

        number = number + jnp.where(place > 0, 1, 0) + jnp.where(place < size - 1, 1, 0)

    def halo_copy(which, target):
        source, destination = ((xsend, xrecv), (ysend, yrecv))[which // 2]
        axis = ("gx", "gy")[which // 2]
        return pltpu.make_async_remote_copy(
            src_ref=source.at[which % 2], dst_ref=destination.at[which % 2],
            send_sem=halo_ssem.at[which], recv_sem=halo_rsem.at[which],
            device_id={axis: target}, device_id_type=pl.DeviceIdType.MESH,
        )

    halos = []
    for which, (place, size) in enumerate(((gx, nx), (gx, nx), (gy, ny), (gy, ny))):
        upward = which % 2 == 0
        copy = halo_copy(which, place + 1 if upward else place - 1)
        sends = place < size - 1 if upward else place > 0
        receives = place > 0 if upward else place < size - 1
        halos.append((copy, sends, receives))

    def up_copy(c):
        return pltpu.make_async_remote_copy(
            src_ref=up_send.at[c], dst_ref=up_recv.at[c], send_sem=up_ssem.at[c], recv_sem=up_rsem.at[c],
            device_id={"gz": gz + 1}, device_id_type=pl.DeviceIdType.MESH,
        )

    def down_copy(c):
        return pltpu.make_async_remote_copy(
            src_ref=down_send.at[c], dst_ref=down_recv.at[c], send_sem=down_ssem.at[c], recv_sem=down_rsem.at[c],
            device_id={"gz": gz - 1}, device_id_type=pl.DeviceIdType.MESH,
        )

    @pl.when(gx == 0)
    def _():
        xrecv[0] = jnp.zeros(xrecv.shape[1:], F32)

    @pl.when(gx == nx - 1)
    def _():
        xrecv[1] = jnp.zeros(xrecv.shape[1:], F32)

    @pl.when(gy == 0)
    def _():
        yrecv[0] = jnp.zeros(yrecv.shape[1:], F32)

    @pl.when(gy == ny - 1)
    def _():
        yrecv[1] = jnp.zeros(yrecv.shape[1:], F32)

    @pl.when(gz == 0)
    def _():
        up_recv[...] = jnp.zeros(up_recv.shape, F32)

    @pl.when(gz == nz - 1)
    def _():
        down_recv[...] = jnp.zeros(down_recv.shape, F32)

    k = lax.broadcasted_iota(jnp.int32, (2 * LANES, LANES), 0)
    j = lax.broadcasted_iota(jnp.int32, (2 * LANES, LANES), 1)
    d = (j - k) & (LANES - 1)
    weight = jnp.where(d == 2, 1.0, 0.0) - jnp.where(d == LANES - 2, 1.0, 0.0)
    weight = weight + jnp.where(d == LANES - 1, 8.0, 0.0) - jnp.where(d == 1, 8.0, 0.0)
    band[...] = weight.astype(BF16)

    for copy in cell_copies:
        copy.wait()

    def pack_x(v, carry):
        for z in range(depth):
            xsend[0, v, 2 * z : 2 * z + 2, :] = cells[v, z, rows - 2 : rows, :]
            xsend[1, v, 2 * z : 2 * z + 2, :] = cells[v, z, 0:2, :]
        return carry

    lax.fori_loop(0, 6, pack_x, 0)
    pl.semaphore_wait(barrier, number)
    for which in (0, 1):
        copy, sends, _ = halos[which]
        pl.when(sends)(copy.start)

    lane = lax.broadcasted_iota(jnp.int32, (CHUNK, LANES), 1)
    pair = lane >> 1

    def pack_y(v, carry):
        low = jnp.zeros((CHUNK, LANES), F32)
        high = low
        for c in range(chunks):
            for z in range(depth):
                slot = CHUNK * c + z
                rolled = cells[v + v // 5, z, c * CHUNK : (c + 1) * CHUNK, :]
                if slot:
                    rolled = pltpu.roll(rolled, 2 * slot, 1)
                low = jnp.where(pair == slot, rolled, low)
                high = jnp.where(pair == (slot - 1) % (LANES // 2), rolled, high)
        ysend[0, v] = high
        ysend[1, v] = low
        return carry

    lax.fori_loop(0, 6, pack_y, 0)
    for which in (2, 3):
        copy, sends, _ = halos[which]
        pl.when(sends)(copy.start)

    matrix_x = [[jx[i, j] for j in range(5)] for i in range(5)]
    matrix_y = [[jy[i, j] for j in range(5)] for i in range(5)]

    def flux(matrix, values, metric):
        factor = metric * SCALE
        return [factor * sum_of([matrix[i][j] * values[j] for j in range(5)]) for i in range(5)]

    def x_plane(z, carry):
        for c in range(chunks):
            part = pl.ds(c * CHUNK, CHUNK)
            values = flux(matrix_x, [cells[j, z, part, :] for j in range(5)], cells[5, z, part, :])
            for i in range(5):
                fx[i, z, 8 + c * CHUNK : 8 + (c + 1) * CHUNK, :] = values[i]
        return carry

    lax.fori_loop(0, depth, x_plane, 0)

    group = min(8, depth)

    def y_planes(step, carry):
        stacks = []
        for z in range(group):
            for c in range(chunks):
                part = pl.ds(c * CHUNK, CHUNK)
                at = step * group + z
                values = flux(matrix_y, [cells[j, at, part, :] for j in range(5)], cells[6, at, part, :])
                for value in values:
                    first = value.astype(BF16)
                    second = (value - first.astype(F32)).astype(BF16)
                    stacks.append(jnp.concatenate([first, second], 1))
        product = jnp.dot(jnp.concatenate(stacks, 0), band[...], preferred_element_type=F32)
        for z in range(group):
            for c in range(chunks):
                for i in range(5):
                    at = ((z * chunks + c) * 5 + i) * CHUNK
                    w[i, step * group + z, c * CHUNK : (c + 1) * CHUNK, :] = product[at : at + CHUNK, :]
        return carry

    lax.fori_loop(0, depth // group, y_planes, 0)

    for copy, _, receives in halos:
        pl.when(receives)(copy.wait_recv)

    for side in range(2):
        values = flux(matrix_x, [xrecv[side, j] for j in range(5)], xrecv[side, 5])
        for i in range(5):
            for z in range(depth):
                start = 6 if side == 0 else 8 + rows
                fx[i, z, start : start + 2, :] = values[i][2 * z : 2 * z + 2, :]

    theirs = [flux(matrix_y, [yrecv[s, j] for j in range(5)], yrecv[s, 5]) for s in range(2)]
    mine = [flux(matrix_y, [ysend[s, j] for j in range(5)], ysend[s, 5]) for s in range(2)]
    odd = (lane & 1) == 1
    upper_pair = (lane & 2) == 2
    for i in range(5):
        high = theirs[0][i] - mine[0][i]
        low = theirs[1][i] - mine[1][i]
        at_start = high - jnp.where(odd, 0.0, 8.0 * pltpu.roll(high, LANES - 1, 1))
        at_end = jnp.where(odd, 8.0 * pltpu.roll(low, 1, 1), 0.0) - low
        at_end = pltpu.roll(at_end, LANES - 4, 1)
        corr[0, i] = jnp.where(upper_pair, at_start, at_end)
        corr[1, i] = jnp.where(upper_pair, at_end, at_start)

    edge = (lane < 2) | (lane >= LANES - 2)

    def force(c):
        base = 8 + c * CHUNK
        part = pl.ds(c * CHUNK, CHUNK)
        for z in range(depth):
            shift = (2 - 2 * CHUNK * c - 2 * z) % LANES
            for i in range(5):
                below2 = fx[i, z, base - 2 : base - 2 + CHUNK, :]
                below1 = fx[i, z, base - 1 : base - 1 + CHUNK, :]
                above1 = fx[i, z, base + 1 : base + 1 + CHUNK, :]
                above2 = fx[i, z, base + 2 : base + 2 + CHUNK, :]
                extra = corr[z % 2, i]
                if shift:
                    extra = pltpu.roll(extra, shift, 1)
                extra = jnp.where(edge, extra, 0.0)
                w[i, z, part, :] = (w[i, z, part, :] + extra) + ((below2 - above2) + 8.0 * (above1 - below1))

    planes = min(4, depth)

    def sweep(plane, carried):
        def several(step, carried):
            for u in range(planes):
                carried = plane(step * planes + u, carried)
            return carried

        return lax.fori_loop(0, depth // planes, several, carried)

    def ahead(c):
        part = pl.ds(c * CHUNK, CHUNK)
        block_copies[0, c].wait()
        block_copies[1, c].wait()

        pl.when(gz > 0)(up_copy(c).wait_recv)

        def plane(z, carried):
            inner = []
            for i in range(5):
                total = w[i, z, part, :]
                for j in range(5):
                    total = total - lo[i, j, z, part, :].astype(F32) * carried[j]
                inner.append(total)
            result_here = []
            for i in range(5):
                total = sum_of([pv[i, j, z, part, :].astype(F32) * inner[j] for j in range(5)])
                w[i, z, part, :] = total
                result_here.append(total)
            return tuple(result_here)

        carried = sweep(plane, tuple(up_recv[c, i] for i in range(5)))
        for i in range(5):
            up_send[c, i] = carried[i]
        pl.when(gz < nz - 1)(up_copy(c).start)

    def out_copy(c):
        part = pl.ds(c * CHUNK, CHUNK)
        return pltpu.make_async_copy(result.at[:, :, part, :], out.at[:, :, part, :], out_sem.at[c])

    def back(c):
        part = pl.ds(c * CHUNK, CHUNK)
        pl.when(gz < nz - 1)(down_copy(c).wait_recv)

        def plane(step, carried):
            z = depth - 1 - step
            new = []
            for i in range(5):
                total = w[i, z, part, :]
                for j in range(5):
                    total = total - up[i, j, z, part, :].astype(F32) * carried[j]
                result[i, z, part, :] = cells[i, z, part, :] + total
                new.append(total)
            return tuple(new)

        carried = sweep(plane, tuple(down_recv[c, i] for i in range(5)))
        for i in range(5):
            down_send[c, i] = carried[i]
        pl.when(gz > 0)(down_copy(c).start)
        out_copy(c).start()

    @pl.when(gz > 0)
    def _():
        for c in range(chunks):
            force(c)

    for c in range(chunks):
        @pl.when(gz == 0)
        def _():
            force(c)

        ahead(c)

        @pl.when(gz == nz - 1)
        def _():
            block_copies[2, c].wait()
            back(c)

    @pl.when(gz < nz - 1)
    def _():
        for c in range(chunks):
            block_copies[2, c].wait()
            back(c)

    for c in range(chunks):
        out_copy(c).wait()
        pl.when(gz < nz - 1)(up_copy(c).wait_send)
        pl.when(gz > 0)(down_copy(c).wait_send)
    for copy, sends, _ in halos:
        pl.when(sends)(copy.wait_send)


def local(fields, metrics, jacobian_x, jacobian_y, pivot_inverse, lower_blocks, upper_blocks):
    _, depth, rows, columns = fields.shape
    chunks = rows // CHUNK
    hbm = pl.BlockSpec(memory_space=pltpu.HBM)
    anywhere = pl.BlockSpec(memory_space=pl.ANY)
    dma = pltpu.SemaphoreType.DMA
    arguments = [
        pltpu.with_memory_space_constraint(argument, pltpu.HBM)
        for argument in (fields, metrics, jacobian_x, jacobian_y, pivot_inverse, lower_blocks, upper_blocks)
    ]
    return pl.pallas_call(
        kernel,
        out_shape=jax.ShapeDtypeStruct(fields.shape, F32),
        in_specs=[hbm] * 7,
        out_specs=anywhere,
        scratch_shapes=[
            pltpu.SMEM((5, 5), F32),
            pltpu.SMEM((5, 5), F32),
            pltpu.VMEM((7, depth, rows, columns), F32),
            pltpu.VMEM(pivot_inverse.shape, BF16),
            pltpu.VMEM(pivot_inverse.shape, BF16),
            pltpu.VMEM(pivot_inverse.shape, BF16),
            pltpu.VMEM((5, depth, rows + 16, columns), F32),
            pltpu.VMEM(fields.shape, F32),
            pltpu.VMEM(fields.shape, F32),
            pltpu.VMEM((2 * LANES, LANES), BF16),
            pltpu.VMEM((2, 6, 2 * depth, columns), F32),
            pltpu.VMEM((2, 6, 2 * depth, columns), F32),
            pltpu.VMEM((2, 6, CHUNK, LANES), F32),
            pltpu.VMEM((2, 6, CHUNK, LANES), F32),
            pltpu.VMEM((2, 5, CHUNK, LANES), F32),
            pltpu.VMEM((chunks, 5, CHUNK, LANES), F32),
            pltpu.VMEM((chunks, 5, CHUNK, LANES), F32),
            pltpu.VMEM((chunks, 5, CHUNK, LANES), F32),
            pltpu.VMEM((chunks, 5, CHUNK, LANES), F32),
            dma((2,)),
            dma((7,)),
            dma((3, chunks)),
            dma((chunks,)),
            dma((4,)),
            dma((4,)),
            dma((chunks,)),
            dma((chunks,)),
            dma((chunks,)),
            dma((chunks,)),
        ],
        compiler_params=pltpu.CompilerParams(
            collective_id=0, has_side_effects=True, vmem_limit_bytes=VMEM_LIMIT
        ),
    )(*arguments)


def solution(mesh):
    cells = P(None, "gz", "gx", "gy")
    blocks = P(None, None, "gz", "gx", "gy")
    return jax.shard_map(
        local, mesh=mesh, in_specs=(cells, cells, P(), P(), blocks, blocks, blocks),
        out_specs=cells, check_vma=False,
    )
```

```python
import jax
import jax.numpy as jnp
from jax import lax
from jax.experimental import pallas as pl
from jax.experimental.pallas import tpu as pltpu
from jax.sharding import PartitionSpec as P

STEP = 0.25
SCALE = -STEP / 12.0
CHUNK = 16
LANES = 128
F32 = jnp.float32
BF16 = jnp.bfloat16
VMEM_LIMIT = 47 * 1024 * 1024


def sum_of(terms):
    total = terms[0]
    for term in terms[1:]:
        total = total + term
    return total


def kernel(
    fields, metrics, jacobian_x, jacobian_y, pivot, lower, upper, out,
    jx, jy, cells, pv, lo, up, product, fx, w, band,
    xsend, xrecv, ysend, yrecv, corr, up_send, up_recv, down_send, down_recv,
    jacobian_sem, cell_sem, block_sem, halo_ssem, halo_rsem, up_ssem, up_rsem, down_ssem, down_rsem,
):
    depth, rows = fields.shape[1], fields.shape[2]
    chunks = rows // CHUNK
    order = (*range(1, chunks - 1), 0, chunks - 1)
    gx, gy, gz = lax.axis_index("gx"), lax.axis_index("gy"), lax.axis_index("gz")
    nx, ny, nz = lax.axis_size("gx"), lax.axis_size("gy"), lax.axis_size("gz")

    cell_copies = []
    for v in range(7):
        source = fields.at[v] if v < 5 else metrics.at[v - 5]
        cell_copies.append(pltpu.make_async_copy(source, cells.at[v], cell_sem.at[v]))
    for v in (0, 1, 2, 3, 4, 6, 5):
        cell_copies[v].start()
    jacobian_copies = [
        pltpu.make_async_copy(jacobian_x, jx, jacobian_sem.at[0]),
        pltpu.make_async_copy(jacobian_y, jy, jacobian_sem.at[1]),
    ]
    for copy in jacobian_copies:
        copy.start()
    block_copies = {}
    for kind, (source, target) in enumerate(((lower, lo), (pivot, pv), (upper, up))):
        for c in range(chunks):
            part = pl.ds(c * CHUNK, CHUNK)
            block_copies[kind, c] = pltpu.make_async_copy(
                source.at[:, :, :, part, :], target.at[:, :, :, part, :], block_sem.at[kind, c]
            )

    barrier = pltpu.get_barrier_semaphore()
    number = jnp.int32(0)
    for axis, place, size in (("gx", gx, nx), ("gy", gy, ny), ("gz", gz, nz)):
        @pl.when(place > 0)
        def _():
            pl.semaphore_signal(barrier, inc=1, device_id={axis: place - 1}, device_id_type=pl.DeviceIdType.MESH)

        @pl.when(place < size - 1)
        def _():
            pl.semaphore_signal(barrier, inc=1, device_id={axis: place + 1}, device_id_type=pl.DeviceIdType.MESH)

        number = number + jnp.where(place > 0, 1, 0) + jnp.where(place < size - 1, 1, 0)

    def halo_copy(which, target):
        source, destination = ((xsend, xrecv), (ysend, yrecv))[which // 2]
        axis = ("gx", "gy")[which // 2]
        return pltpu.make_async_remote_copy(
            src_ref=source.at[which % 2], dst_ref=destination.at[which % 2],
            send_sem=halo_ssem.at[which], recv_sem=halo_rsem.at[which],
            device_id={axis: target}, device_id_type=pl.DeviceIdType.MESH,
        )

    halos = []
    for which, (place, size) in enumerate(((gx, nx), (gx, nx), (gy, ny), (gy, ny))):
        upward = which % 2 == 0
        copy = halo_copy(which, place + 1 if upward else place - 1)
        sends = place < size - 1 if upward else place > 0
        receives = place > 0 if upward else place < size - 1
        halos.append((copy, sends, receives))

    def up_copy(c):
        return pltpu.make_async_remote_copy(
            src_ref=up_send.at[c], dst_ref=up_recv.at[c], send_sem=up_ssem.at[c], recv_sem=up_rsem.at[c],
            device_id={"gz": gz + 1}, device_id_type=pl.DeviceIdType.MESH,
        )

    def down_copy(c):
        return pltpu.make_async_remote_copy(
            src_ref=down_send.at[c], dst_ref=down_recv.at[c], send_sem=down_ssem.at[c], recv_sem=down_rsem.at[c],
            device_id={"gz": gz - 1}, device_id_type=pl.DeviceIdType.MESH,
        )

    @pl.when(gx == 0)
    def _():
        xrecv[0] = jnp.zeros(xrecv.shape[1:], F32)

    @pl.when(gx == nx - 1)
    def _():
        xrecv[1] = jnp.zeros(xrecv.shape[1:], F32)

    @pl.when(gy == 0)
    def _():
        yrecv[0] = jnp.zeros(yrecv.shape[1:], F32)

    @pl.when(gy == ny - 1)
    def _():
        yrecv[1] = jnp.zeros(yrecv.shape[1:], F32)

    @pl.when(gz == 0)
    def _():
        up_recv[...] = jnp.zeros(up_recv.shape, F32)

    @pl.when(gz == nz - 1)
    def _():
        down_recv[...] = jnp.zeros(down_recv.shape, F32)

    k = lax.broadcasted_iota(jnp.int32, (2 * LANES, LANES), 0)
    j = lax.broadcasted_iota(jnp.int32, (2 * LANES, LANES), 1)
    d = (j - k) & (LANES - 1)
    weight = jnp.where(d == 2, 1.0, 0.0) - jnp.where(d == LANES - 2, 1.0, 0.0)
    weight = weight + jnp.where(d == LANES - 1, 8.0, 0.0) - jnp.where(d == 1, 8.0, 0.0)
    band[...] = weight.astype(BF16)

    lane = lax.broadcasted_iota(jnp.int32, (CHUNK, LANES), 1)
    pair = lane >> 1

    for v in range(6):
        cell = v + v // 5
        cell_copies[cell].wait()
        low = jnp.zeros((CHUNK, LANES), F32)
        high = low
        for c in range(chunks):
            for z in range(depth):
                slot = CHUNK * c + z
                rolled = cells[cell, z, c * CHUNK : (c + 1) * CHUNK, :]
                if slot:
                    rolled = pltpu.roll(rolled, 2 * slot, 1)
                low = jnp.where(pair == slot, rolled, low)
                high = jnp.where(pair == (slot - 1) % (LANES // 2), rolled, high)
        ysend[0, v] = high
        ysend[1, v] = low

    pl.semaphore_wait(barrier, number)
    for which in (2, 3):
        copy, sends, _ = halos[which]
        pl.when(sends)(copy.start)
    cell_copies[5].wait()
    for c in order[: chunks // 2]:
        block_copies[0, c].start()
        block_copies[1, c].start()

    def pack_x(v, carry):
        for z in range(depth):
            xsend[0, v, 2 * z : 2 * z + 2, :] = cells[v, z, rows - 2 : rows, :]
            xsend[1, v, 2 * z : 2 * z + 2, :] = cells[v, z, 0:2, :]
        return carry

    lax.fori_loop(0, 6, pack_x, 0)
    for which in (0, 1):
        copy, sends, _ = halos[which]
        pl.when(sends)(copy.start)
    for copy in jacobian_copies:
        copy.wait()

    matrix_x = [[jx[i, j] for j in range(5)] for i in range(5)]
    matrix_y = [[jy[i, j] for j in range(5)] for i in range(5)]

    def flux(matrix, values, metric):
        factor = metric * SCALE
        return [factor * sum_of([matrix[i][j] * values[j] for j in range(5)]) for i in range(5)]

    def x_plane(z, carry):
        for i in range(5):
            fx[i, z, 0:8, :] = jnp.zeros((8, LANES), F32)
            fx[i, z, rows + 8 : rows + 16, :] = jnp.zeros((8, LANES), F32)
        for c in range(chunks):
            part = pl.ds(c * CHUNK, CHUNK)
            values = flux(matrix_x, [cells[j, z, part, :] for j in range(5)], cells[5, z, part, :])
            for i in range(5):
                fx[i, z, 8 + c * CHUNK : 8 + (c + 1) * CHUNK, :] = values[i]
        return carry

    lax.fori_loop(0, depth, x_plane, 0)
    for c in order[chunks // 2 :]:
        block_copies[0, c].start()
        block_copies[1, c].start()

    group = min(8, depth)

    def y_planes(step, carry):
        stacks = []
        for z in range(group):
            for c in range(chunks):
                part = pl.ds(c * CHUNK, CHUNK)
                at = step * group + z
                values = flux(matrix_y, [cells[j, at, part, :] for j in range(5)], cells[6, at, part, :])
                for value in values:
                    first = value.astype(BF16)
                    second = (value - first.astype(F32)).astype(BF16)
                    stacks.append(jnp.concatenate([first, second], 1))
        derived = jnp.dot(jnp.concatenate(stacks, 0), band[...], preferred_element_type=F32)
        for z in range(group):
            for c in range(chunks):
                for i in range(5):
                    at = ((z * chunks + c) * 5 + i) * CHUNK
                    plane = step * group + z
                    base = 8 + c * CHUNK
                    below2, below1, above1, above2 = (
                        fx[i, plane, base + d : base + d + CHUNK, :] for d in (-2, -1, 1, 2)
                    )
                    along_x = (below2 - above2) + 8.0 * (above1 - below1)
                    w[i, plane, c * CHUNK : (c + 1) * CHUNK, :] = derived[at : at + CHUNK, :] + along_x
        return carry

    lax.fori_loop(0, depth // group, y_planes, 0)

    for c in order:
        block_copies[2, c].start()

    odd = (lane & 1) == 1
    upper_pair = (lane & 2) == 2
    edge = (lane < 2) | (lane >= LANES - 2)
    mine = [flux(matrix_y, [ysend[s, j] for j in range(5)], ysend[s, 5]) for s in range(2)]
    for copy, _, receives in halos[2:]:
        pl.when(receives)(copy.wait_recv)
    theirs = [flux(matrix_y, [yrecv[s, j] for j in range(5)], yrecv[s, 5]) for s in range(2)]
    for i in range(5):
        high = theirs[0][i] - mine[0][i]
        low = theirs[1][i] - mine[1][i]
        at_start = high - jnp.where(odd, 0.0, 8.0 * pltpu.roll(high, LANES - 1, 1))
        at_end = jnp.where(odd, 8.0 * pltpu.roll(low, 1, 1), 0.0) - low
        at_end = pltpu.roll(at_end, LANES - 4, 1)
        corr[0, i] = jnp.where(upper_pair, at_start, at_end)
        corr[1, i] = jnp.where(upper_pair, at_end, at_start)

    def add_x_halo(side):
        copy, _, receives = halos[side]
        pl.when(receives)(copy.wait_recv)
        values = flux(matrix_x, [xrecv[side, j] for j in range(5)], xrecv[side, 5])
        odd_row = (lax.broadcasted_iota(jnp.int32, (2 * depth, LANES), 0) & 1) == 1
        for i in range(5):
            if side == 0:
                extra = values[i] - jnp.where(odd_row, 0.0, 8.0 * pltpu.roll(values[i], 2 * depth - 1, 0))
                start = 0
            else:
                extra = jnp.where(odd_row, 8.0 * pltpu.roll(values[i], 1, 0), 0.0) - values[i]
                start = rows - 2
            for z in range(depth):
                w[i, z, start : start + 2, :] = w[i, z, start : start + 2, :] + extra[2 * z : 2 * z + 2, :]

    planes = min(4, depth)

    def sweep(plane, carried):
        def several(step, carried):
            for u in range(planes):
                carried = plane(step * planes + u, carried)
            return carried

        return lax.fori_loop(0, depth // planes, several, carried)

    def ahead(c):
        part = pl.ds(c * CHUNK, CHUNK)
        block_copies[0, c].wait()
        block_copies[1, c].wait()

        pl.when(gz > 0)(up_copy(c).wait_recv)

        def plane(z, carried):
            inner = []
            shift = (2 - 2 * CHUNK * c - 2 * z) % LANES
            for i in range(5):
                extra = corr[z % 2, i]
                if shift:
                    extra = pltpu.roll(extra, shift, 1)
                total = w[i, z, part, :] + jnp.where(edge, extra, 0.0)
                for j in range(5):
                    total = total - lo[i, j, z, part, :].astype(F32) * carried[j]
                inner.append(total)
            result_here = []
            for i in range(5):
                total = sum_of([pv[i, j, z, part, :].astype(F32) * inner[j] for j in range(5)])
                w[i, z, part, :] = total
                result_here.append(total)
            return tuple(result_here)

        carried = tuple(up_recv[c, i] for i in range(5))
        for z in range(depth):
            carried = plane(z, carried)
        for i in range(5):
            up_send[c, i] = carried[i]
        pl.when(gz < nz - 1)(up_copy(c).start)

    def prepare(c):
        part = pl.ds(c * CHUNK, CHUNK)
        block_copies[0, c].wait()
        block_copies[1, c].wait()
        for z in range(depth):
            shift = (2 - 2 * CHUNK * c - 2 * z) % LANES
            source = []
            for i in range(5):
                extra = corr[z % 2, i]
                if shift:
                    extra = pltpu.roll(extra, shift, 1)
                source.append(w[i, z, part, :] + jnp.where(edge, extra, 0.0))
            for i in range(5):
                w[i, z, part, :] = sum_of([pv[i, j, z, part, :].astype(F32) * source[j] for j in range(5)])

        def plane(z, carry):
            for j in range(5):
                column = [lo[k, j, z, part, :].astype(F32) for k in range(5)]
                for i in range(5):
                    product[i, j, z, part, :] = sum_of(
                        [pv[i, k, z, part, :].astype(F32) * column[k] for k in range(5)]
                    )
            return carry

        lax.fori_loop(0, depth, plane, 0)

    def ahead_prepared(c):
        part = pl.ds(c * CHUNK, CHUNK)
        up_copy(c).wait_recv()

        def plane(z, carried):
            new = []
            for i in range(5):
                total = w[i, z, part, :]
                for j in range(5):
                    total = total - product[i, j, z, part, :] * carried[j]
                w[i, z, part, :] = total
                new.append(total)
            return tuple(new)

        sweep(plane, tuple(up_recv[c, i] for i in range(5)))

    def back(c):
        part = pl.ds(c * CHUNK, CHUNK)
        pl.when(gz < nz - 1)(down_copy(c).wait_recv)

        def plane(step, carried):
            z = depth - 1 - step
            new = []
            for i in range(5):
                total = w[i, z, part, :]
                for j in range(5):
                    total = total - up[i, j, z, part, :].astype(F32) * carried[j]
                out[i, z, part, :] = cells[i, z, part, :] + total
                new.append(total)
            return tuple(new)

        carried = sweep(plane, tuple(down_recv[c, i] for i in range(5)))
        for i in range(5):
            down_send[c, i] = carried[i]
        pl.when(gz > 0)(down_copy(c).start)

    @pl.when(gz < nz - 1)
    def _():
        for c in order:
            if c == 0:
                add_x_halo(0)
            if c == chunks - 1:
                add_x_halo(1)
            ahead(c)
        for c in order:
            block_copies[2, c].wait()
            back(c)

    @pl.when(gz == nz - 1)
    def _():
        add_x_halo(0)
        add_x_halo(1)
        for c in order:
            prepare(c)
        for c in order:
            ahead_prepared(c)
            block_copies[2, c].wait()
            back(c)

    for c in range(chunks):
        pl.when(gz < nz - 1)(up_copy(c).wait_send)
        pl.when(gz > 0)(down_copy(c).wait_send)
    for copy, sends, _ in halos:
        pl.when(sends)(copy.wait_send)


def local(fields, metrics, jacobian_x, jacobian_y, pivot_inverse, lower_blocks, upper_blocks):
    _, depth, rows, columns = fields.shape
    chunks = rows // CHUNK
    hbm = pl.BlockSpec(memory_space=pltpu.HBM)
    anywhere = pl.BlockSpec(memory_space=pl.ANY)
    dma = pltpu.SemaphoreType.DMA
    arguments = [
        pltpu.with_memory_space_constraint(argument, pltpu.HBM)
        for argument in (fields, metrics, jacobian_x, jacobian_y, pivot_inverse, lower_blocks, upper_blocks)
    ]
    return pl.pallas_call(
        kernel,
        out_shape=jax.ShapeDtypeStruct(fields.shape, F32),
        in_specs=[hbm] * 7,
        out_specs=pl.BlockSpec(memory_space=pltpu.VMEM),
        scratch_shapes=[
            pltpu.SMEM((5, 5), F32),
            pltpu.SMEM((5, 5), F32),
            pltpu.VMEM((7, depth, rows, columns), F32),
            pltpu.VMEM(pivot_inverse.shape, BF16),
            pltpu.VMEM(pivot_inverse.shape, BF16),
            pltpu.VMEM(pivot_inverse.shape, BF16),
            pltpu.VMEM(pivot_inverse.shape, F32),
            pltpu.VMEM((5, depth, rows + 16, columns), F32),
            pltpu.VMEM(fields.shape, F32),
            pltpu.VMEM((2 * LANES, LANES), BF16),
            pltpu.VMEM((2, 6, 2 * depth, columns), F32),
            pltpu.VMEM((2, 6, 2 * depth, columns), F32),
            pltpu.VMEM((2, 6, CHUNK, LANES), F32),
            pltpu.VMEM((2, 6, CHUNK, LANES), F32),
            pltpu.VMEM((2, 5, CHUNK, LANES), F32),
            pltpu.VMEM((chunks, 5, CHUNK, LANES), F32),
            pltpu.VMEM((chunks, 5, CHUNK, LANES), F32),
            pltpu.VMEM((chunks, 5, CHUNK, LANES), F32),
            pltpu.VMEM((chunks, 5, CHUNK, LANES), F32),
            dma((2,)),
            dma((7,)),
            dma((3, chunks)),
            dma((4,)),
            dma((4,)),
            dma((chunks,)),
            dma((chunks,)),
            dma((chunks,)),
            dma((chunks,)),
        ],
        compiler_params=pltpu.CompilerParams(
            collective_id=0, has_side_effects=True, vmem_limit_bytes=VMEM_LIMIT
        ),
    )(*arguments)


def solution(mesh):
    cells = P(None, "gz", "gx", "gy")
    blocks = P(None, None, "gz", "gx", "gy")
    return jax.shard_map(
        local, mesh=mesh, in_specs=(cells, cells, P(), P(), blocks, blocks, blocks),
        out_specs=cells, check_vma=False,
    )
```

```python
import jax
import jax.numpy as jnp
from jax import lax
from jax.experimental import pallas as pl
from jax.experimental.pallas import tpu as pltpu
from jax.sharding import PartitionSpec as P

STEP = 0.25
SCALE = -STEP / 12.0
CHUNK = 16
LANES = 128
F32 = jnp.float32
BF16 = jnp.bfloat16
VMEM_LIMIT = 47 * 1024 * 1024


def sum_of(terms):
    total = terms[0]
    for term in terms[1:]:
        total = total + term
    return total


def kernel(
    fields, metrics, jacobian_x, jacobian_y, pivot, lower, upper, out,
    jx, jy, cells, pv, lo, up, product, fx, w, band,
    xsend, xrecv, ysend, yrecv, corr, up_send, up_recv, down_send, down_recv,
    jacobian_sem, cell_sem, block_sem, halo_ssem, halo_rsem, up_ssem, up_rsem, down_ssem, down_rsem,
):
    depth, rows = fields.shape[1], fields.shape[2]
    chunks = rows // CHUNK
    order = (*range(1, chunks), 0)
    gx, gy, gz = lax.axis_index("gx"), lax.axis_index("gy"), lax.axis_index("gz")
    nx, ny, nz = lax.axis_size("gx"), lax.axis_size("gy"), lax.axis_size("gz")

    barrier = pltpu.get_barrier_semaphore()
    number = jnp.int32(0)
    for axis, place, size in (("gx", gx, nx), ("gy", gy, ny), ("gz", gz, nz)):
        @pl.when(place > 0)
        def _():
            pl.semaphore_signal(barrier, inc=1, device_id={axis: place - 1}, device_id_type=pl.DeviceIdType.MESH)

        @pl.when(place < size - 1)
        def _():
            pl.semaphore_signal(barrier, inc=1, device_id={axis: place + 1}, device_id_type=pl.DeviceIdType.MESH)

        number = number + jnp.where(place > 0, 1, 0) + jnp.where(place < size - 1, 1, 0)

    cell_copies = []
    for v in range(7):
        source = fields.at[v] if v < 5 else metrics.at[v - 5]
        cell_copies.append(pltpu.make_async_copy(source, cells.at[v], cell_sem.at[v]))
    for v in (0, 1, 2, 3, 4, 6, 5):
        cell_copies[v].start()
    jacobian_copies = [
        pltpu.make_async_copy(jacobian_x, jx, jacobian_sem.at[0]),
        pltpu.make_async_copy(jacobian_y, jy, jacobian_sem.at[1]),
    ]
    for copy in jacobian_copies:
        copy.start()
    def block_copy(kind, c):
        part = pl.ds(c * CHUNK if isinstance(c, int) else pl.multiple_of(c * CHUNK, CHUNK), CHUNK)
        source, target = ((lower, lo), (pivot, pv), (upper, up))[kind]
        return pltpu.make_async_copy(
            source.at[:, :, :, part, :], target.at[:, :, :, part, :], block_sem.at[kind, c]
        )

    def halo_copy(which, target):
        source, destination = ((xsend, xrecv), (ysend, yrecv))[which // 2]
        axis = ("gx", "gy")[which // 2]
        return pltpu.make_async_remote_copy(
            src_ref=source.at[which % 2], dst_ref=destination.at[which % 2],
            send_sem=halo_ssem.at[which], recv_sem=halo_rsem.at[which],
            device_id={axis: target}, device_id_type=pl.DeviceIdType.MESH,
        )

    halos = []
    for which, (place, size) in enumerate(((gx, nx), (gx, nx), (gy, ny), (gy, ny))):
        upward = which % 2 == 0
        copy = halo_copy(which, place + 1 if upward else place - 1)
        sends = place < size - 1 if upward else place > 0
        receives = place > 0 if upward else place < size - 1
        halos.append((copy, sends, receives))

    def up_copy(c):
        return pltpu.make_async_remote_copy(
            src_ref=up_send.at[c], dst_ref=up_recv.at[c], send_sem=up_ssem.at[c], recv_sem=up_rsem.at[c],
            device_id={"gz": gz + 1}, device_id_type=pl.DeviceIdType.MESH,
        )

    def down_copy(c):
        return pltpu.make_async_remote_copy(
            src_ref=down_send.at[c], dst_ref=down_recv.at[c], send_sem=down_ssem.at[c], recv_sem=down_rsem.at[c],
            device_id={"gz": gz - 1}, device_id_type=pl.DeviceIdType.MESH,
        )

    @pl.when(gx == 0)
    def _():
        xrecv[0] = jnp.zeros(xrecv.shape[1:], F32)

    @pl.when(gx == nx - 1)
    def _():
        xrecv[1] = jnp.zeros(xrecv.shape[1:], F32)

    @pl.when(gy == 0)
    def _():
        yrecv[0] = jnp.zeros(yrecv.shape[1:], F32)

    @pl.when(gy == ny - 1)
    def _():
        yrecv[1] = jnp.zeros(yrecv.shape[1:], F32)

    @pl.when(gz == 0)
    def _():
        up_recv[...] = jnp.zeros(up_recv.shape, F32)

    @pl.when(gz == nz - 1)
    def _():
        down_recv[...] = jnp.zeros(down_recv.shape, F32)

    k = lax.broadcasted_iota(jnp.int32, (2 * LANES, LANES), 0)
    j = lax.broadcasted_iota(jnp.int32, (2 * LANES, LANES), 1)
    d = (j - k) & (LANES - 1)
    weight = jnp.where(d == 2, 1.0, 0.0) - jnp.where(d == LANES - 2, 1.0, 0.0)
    weight = weight + jnp.where(d == LANES - 1, 8.0, 0.0) - jnp.where(d == 1, 8.0, 0.0)
    band[...] = weight.astype(BF16)

    lane = lax.broadcasted_iota(jnp.int32, (CHUNK, LANES), 1)
    pair = lane >> 1

    def pack_y(v, cell):
        low = jnp.zeros((CHUNK, LANES), F32)
        high = low
        for c in range(chunks):
            for z in range(depth):
                slot = CHUNK * c + z
                rolled = cells[cell, z, c * CHUNK : (c + 1) * CHUNK, :]
                if slot:
                    rolled = pltpu.roll(rolled, 2 * slot, 1)
                low = jnp.where(pair == slot, rolled, low)
                high = jnp.where(pair == (slot - 1) % (LANES // 2), rolled, high)
        ysend[0, v] = high
        ysend[1, v] = low

    def pack_field(v, carry):
        pltpu.make_async_copy(fields.at[v], cells.at[v], cell_sem.at[v]).wait()
        pack_y(v, v)
        return carry

    lax.fori_loop(0, 5, pack_field, 0)
    cell_copies[6].wait()
    pack_y(5, 6)

    pl.semaphore_wait(barrier, number)
    for which in (2, 3):
        copy, sends, _ = halos[which]
        pl.when(sends)(copy.start)
    cell_copies[5].wait()
    for c in order[: chunks // 2]:
        block_copy(0, c).start()
        block_copy(1, c).start()

    def pack_x(v, carry):
        for z in range(depth):
            xsend[0, v, 2 * z : 2 * z + 2, :] = cells[v, z, rows - 2 : rows, :]
            xsend[1, v, 2 * z : 2 * z + 2, :] = cells[v, z, 0:2, :]
        return carry

    lax.fori_loop(0, 6, pack_x, 0)
    for which in (0, 1):
        copy, sends, _ = halos[which]
        pl.when(sends)(copy.start)
    for copy in jacobian_copies:
        copy.wait()

    matrix_x = [[jx[i, j] for j in range(5)] for i in range(5)]
    matrix_y = [[jy[i, j] for j in range(5)] for i in range(5)]

    def flux(matrix, values, metric):
        factor = metric * SCALE
        return [factor * sum_of([matrix[i][j] * values[j] for j in range(5)]) for i in range(5)]

    def x_plane(z, carry):
        for i in range(5):
            fx[i, z, 0:8, :] = jnp.zeros((8, LANES), F32)
            fx[i, z, rows + 8 : rows + 16, :] = jnp.zeros((8, LANES), F32)
        for c in range(chunks):
            part = pl.ds(c * CHUNK, CHUNK)
            values = flux(matrix_x, [cells[j, z, part, :] for j in range(5)], cells[5, z, part, :])
            for i in range(5):
                fx[i, z, 8 + c * CHUNK : 8 + (c + 1) * CHUNK, :] = values[i]
        return carry

    lax.fori_loop(0, depth, x_plane, 0)
    for c in order[chunks // 2 :]:
        block_copy(0, c).start()
        block_copy(1, c).start()

    group = min(8, depth)

    def y_planes(step, carry):
        stacks = []
        for z in range(group):
            for c in range(chunks):
                part = pl.ds(c * CHUNK, CHUNK)
                at = step * group + z
                values = flux(matrix_y, [cells[j, at, part, :] for j in range(5)], cells[6, at, part, :])
                for value in values:
                    first = value.astype(BF16)
                    second = (value - first.astype(F32)).astype(BF16)
                    stacks.append(jnp.concatenate([first, second], 1))
        derived = jnp.dot(jnp.concatenate(stacks, 0), band[...], preferred_element_type=F32)
        for z in range(group):
            for c in range(chunks):
                for i in range(5):
                    at = ((z * chunks + c) * 5 + i) * CHUNK
                    plane = step * group + z
                    base = 8 + c * CHUNK
                    below2, below1, above1, above2 = (
                        fx[i, plane, base + d : base + d + CHUNK, :] for d in (-2, -1, 1, 2)
                    )
                    along_x = (below2 - above2) + 8.0 * (above1 - below1)
                    w[i, plane, c * CHUNK : (c + 1) * CHUNK, :] = derived[at : at + CHUNK, :] + along_x
        return carry

    lax.fori_loop(0, depth // group, y_planes, 0)

    for c in order:
        block_copy(2, c).start()

    def each_chunk(body):
        def step(k, carry):
            body(lax.rem(k + 1, chunks))
            return carry

        lax.fori_loop(0, chunks, step, 0)

    def multiply(c):
        part = pl.ds(pl.multiple_of(c * CHUNK, CHUNK), CHUNK)
        block_copy(0, c).wait()
        block_copy(1, c).wait()

        def plane(z, carry):
            for j in range(5):
                column = [lo[k, j, z, part, :].astype(F32) for k in range(5)]
                for i in range(5):
                    product[i, j, z, part, :] = sum_of(
                        [pv[i, k, z, part, :].astype(F32) * column[k] for k in range(5)]
                    )
            return carry

        lax.fori_loop(0, depth, plane, 0)

    prepares = max(nz - 2, 1)

    @pl.when(gz >= prepares)
    def _():
        each_chunk(multiply)

    odd = (lane & 1) == 1
    upper_pair = (lane & 2) == 2
    edge = (lane < 2) | (lane >= LANES - 2)
    mine = [flux(matrix_y, [ysend[s, j] for j in range(5)], ysend[s, 5]) for s in range(2)]
    for copy, _, receives in halos[2:]:
        pl.when(receives)(copy.wait_recv)
    theirs = [flux(matrix_y, [yrecv[s, j] for j in range(5)], yrecv[s, 5]) for s in range(2)]
    for i in range(5):
        high = theirs[0][i] - mine[0][i]
        low = theirs[1][i] - mine[1][i]
        at_start = high - jnp.where(odd, 0.0, 8.0 * pltpu.roll(high, LANES - 1, 1))
        at_end = jnp.where(odd, 8.0 * pltpu.roll(low, 1, 1), 0.0) - low
        at_end = pltpu.roll(at_end, LANES - 4, 1)
        first = (2 - 2 * CHUNK * order[0]) % LANES
        corr[0, i] = pltpu.roll(jnp.where(upper_pair, at_start, at_end), first, 1)
        corr[1, i] = pltpu.roll(jnp.where(upper_pair, at_end, at_start), (first - 2) % LANES, 1)

    def add_x_halo(side):
        copy, _, receives = halos[side]
        pl.when(receives)(copy.wait_recv)
        values = flux(matrix_x, [xrecv[side, j] for j in range(5)], xrecv[side, 5])
        odd_row = (lax.broadcasted_iota(jnp.int32, (2 * depth, LANES), 0) & 1) == 1
        for i in range(5):
            if side == 0:
                extra = values[i] - jnp.where(odd_row, 0.0, 8.0 * pltpu.roll(values[i], 2 * depth - 1, 0))
                start = 0
            else:
                extra = jnp.where(odd_row, 8.0 * pltpu.roll(values[i], 1, 0), 0.0) - values[i]
                start = rows - 2
            for z in range(depth):
                w[i, z, start : start + 2, :] = w[i, z, start : start + 2, :] + extra[2 * z : 2 * z + 2, :]

    planes = min(8, depth)

    def forcing(z, u, part):
        source = []
        for i in range(5):
            extra = corr[u % 2, i]
            corr[u % 2, i] = pltpu.roll(extra, LANES - 4, 1)
            source.append(w[i, z, part, :] + jnp.where(edge, extra, 0.0))
        return source

    def next_chunk():
        turn = (2 * depth - 2 * CHUNK) % LANES
        if turn:
            for p in range(2):
                for i in range(5):
                    corr[p, i] = pltpu.roll(corr[p, i], turn, 1)

    def sweep(plane, carried):
        def several(step, carried):
            for u in range(planes):
                carried = plane(step * planes + u, u, carried)
            return carried

        return lax.fori_loop(0, depth // planes, several, carried)

    def ahead(c):
        part = pl.ds(pl.multiple_of(c * CHUNK, CHUNK), CHUNK)
        block_copy(0, c).wait()
        block_copy(1, c).wait()

        pl.when(gz > 0)(up_copy(c).wait_recv)

        def plane(z, u, carried):
            source = forcing(z, u, part)
            inner = []
            for i in range(5):
                total = source[i]
                for j in range(5):
                    total = total - lo[i, j, z, part, :].astype(F32) * carried[j]
                inner.append(total)
            new = []
            for i in range(5):
                total = sum_of([pv[i, j, z, part, :].astype(F32) * inner[j] for j in range(5)])
                w[i, z, part, :] = total
                new.append(total)
            return tuple(new)

        carried = sweep(plane, tuple(up_recv[c, i] for i in range(5)))
        for i in range(5):
            up_send[c, i] = carried[i]
        pl.when(gz < nz - 1)(up_copy(c).start)
        next_chunk()

    def prepare(c):
        part = pl.ds(pl.multiple_of(c * CHUNK, CHUNK), CHUNK)

        def scale(z, u, carry):
            source = forcing(z, u, part)
            for i in range(5):
                w[i, z, part, :] = sum_of([pv[i, j, z, part, :].astype(F32) * source[j] for j in range(5)])
            return carry

        sweep(scale, 0)
        next_chunk()

    def ahead_prepared(c):
        part = pl.ds(pl.multiple_of(c * CHUNK, CHUNK), CHUNK)
        up_copy(c).wait_recv()

        def plane(z, u, carried):
            new = []
            for i in range(5):
                total = w[i, z, part, :]
                for j in range(5):
                    total = total - product[i, j, z, part, :] * carried[j]
                w[i, z, part, :] = total
                new.append(total)
            return tuple(new)

        carried = sweep(plane, tuple(up_recv[c, i] for i in range(5)))
        for i in range(5):
            up_send[c, i] = carried[i]
        pl.when(gz < nz - 1)(up_copy(c).start)

    def back(c):
        part = pl.ds(pl.multiple_of(c * CHUNK, CHUNK), CHUNK)
        pl.when(gz < nz - 1)(down_copy(c).wait_recv)

        def plane(step, u, carried):
            z = depth - 1 - step
            new = []
            for i in range(5):
                total = w[i, z, part, :]
                for j in range(5):
                    total = total - up[i, j, z, part, :].astype(F32) * carried[j]
                out[i, z, part, :] = cells[i, z, part, :] + total
                new.append(total)
            return tuple(new)

        carried = sweep(plane, tuple(down_recv[c, i] for i in range(5)))
        for i in range(5):
            down_send[c, i] = carried[i]
        pl.when(gz > 0)(down_copy(c).start)

    @pl.when(gz < prepares)
    def _():
        def forward(c):
            @pl.when(c == chunks - 1)
            def _():
                add_x_halo(1)

            @pl.when(c == 0)
            def _():
                add_x_halo(0)

            ahead(c)

        each_chunk(forward)

    @pl.when(gz >= prepares)
    def _():
        def both(c):
            ahead_prepared(c)

            @pl.when(gz == nz - 1)
            def _():
                block_copy(2, c).wait()
                back(c)

        add_x_halo(0)
        add_x_halo(1)
        each_chunk(prepare)
        each_chunk(both)

    @pl.when(gz < nz - 1)
    def _():
        def backward(c):
            block_copy(2, c).wait()
            back(c)

        each_chunk(backward)

    for c in range(chunks):
        pl.when(gz < nz - 1)(up_copy(c).wait_send)
        pl.when(gz > 0)(down_copy(c).wait_send)
    for copy, sends, _ in halos:
        pl.when(sends)(copy.wait_send)


def local(fields, metrics, jacobian_x, jacobian_y, pivot_inverse, lower_blocks, upper_blocks):
    _, depth, rows, columns = fields.shape
    chunks = rows // CHUNK
    hbm = pl.BlockSpec(memory_space=pltpu.HBM)
    anywhere = pl.BlockSpec(memory_space=pl.ANY)
    dma = pltpu.SemaphoreType.DMA
    arguments = [
        pltpu.with_memory_space_constraint(argument, pltpu.HBM)
        for argument in (fields, metrics, jacobian_x, jacobian_y, pivot_inverse, lower_blocks, upper_blocks)
    ]
    return pl.pallas_call(
        kernel,
        out_shape=jax.ShapeDtypeStruct(fields.shape, F32),
        in_specs=[hbm] * 7,
        out_specs=pl.BlockSpec(memory_space=pltpu.VMEM),
        scratch_shapes=[
            pltpu.SMEM((5, 5), F32),
            pltpu.SMEM((5, 5), F32),
            pltpu.VMEM((7, depth, rows, columns), F32),
            pltpu.VMEM(pivot_inverse.shape, BF16),
            pltpu.VMEM(pivot_inverse.shape, BF16),
            pltpu.VMEM(pivot_inverse.shape, BF16),
            pltpu.VMEM(pivot_inverse.shape, F32),
            pltpu.VMEM((5, depth, rows + 16, columns), F32),
            pltpu.VMEM(fields.shape, F32),
            pltpu.VMEM((2 * LANES, LANES), BF16),
            pltpu.VMEM((2, 6, 2 * depth, columns), F32),
            pltpu.VMEM((2, 6, 2 * depth, columns), F32),
            pltpu.VMEM((2, 6, CHUNK, LANES), F32),
            pltpu.VMEM((2, 6, CHUNK, LANES), F32),
            pltpu.VMEM((2, 5, CHUNK, LANES), F32),
            pltpu.VMEM((chunks, 5, CHUNK, LANES), F32),
            pltpu.VMEM((chunks, 5, CHUNK, LANES), F32),
            pltpu.VMEM((chunks, 5, CHUNK, LANES), F32),
            pltpu.VMEM((chunks, 5, CHUNK, LANES), F32),
            dma((2,)),
            dma((7,)),
            dma((3, chunks)),
            dma((4,)),
            dma((4,)),
            dma((chunks,)),
            dma((chunks,)),
            dma((chunks,)),
            dma((chunks,)),
        ],
        compiler_params=pltpu.CompilerParams(
            collective_id=0, has_side_effects=True, vmem_limit_bytes=VMEM_LIMIT
        ),
    )(*arguments)


def solution(mesh):
    cells = P(None, "gz", "gx", "gy")
    blocks = P(None, None, "gz", "gx", "gy")
    return jax.shard_map(
        local, mesh=mesh, in_specs=(cells, cells, P(), P(), blocks, blocks, blocks),
        out_specs=cells, check_vma=False,
    )
```
